256 devices in a mesh: win: 32 (over z, x), dep: 8 (over y, core).
Axes of the slice: x: 4, y: 4, z: 8, core: 2. Of those that a mesh axis runs over, the one named last changes fastest.
Arguments:
- slots: bfloat16 [4096, 64, 4096], P('win', 'dep'), may hold values from -4 to 4
- slot_window: int32 [4096, 1], P('win'), may hold values from 0 to 127; in each aligned block of 128 rows (0 to 127, 128 to 255, ...) at most 2 rows name the same one
- first_image: bfloat16 [128, 64, 4096], P('win', 'dep'), may hold values from -6 to 6
Outputs:
- filters: float32 [128, 125], P('win')
The draws below stay inside these ranges and needn't reach their ends.
Inputs may be any that keep to these rules, and one draw needn't show every extreme that they name: `slot_window`: in each aligned block of 128 rows (the slots of one index of win) no window is named by more than 2 rows, a bound that some block reaches; every window is named somewhere.
All inputs are finite; a program needn't handle non-finite values.
Results may differ from the reference program's by a relative error of at most 0.0056.
Values may be sent and summed in bfloat16 or wider, within the bound.
A program may use at most 128 MiB of HBM per device.

```python
import math
import jax
import jax.numpy as jnp
import numpy as np
from jax import lax

WL = 64
CAP = 2
REACH = 2
LAGS = 125
WINDOWS = 128
DEPTH = 64
SLOTS_DEV = 128
SLOTS = 4096
N_WIN = 32


def draw_slots(key, part):
    key = jax.random.fold_in(key, 11)
    first_key = jax.random.fold_in(key, 0)
    shape = (SLOTS, DEPTH, WL * WL)
    base = 0.5 * jax.random.normal(first_key, shape, jnp.float32)
    mixed = base + 0.4 * jnp.roll(base, 1, axis=2) + 0.3 * jnp.roll(base, 1, axis=1)
    return jnp.clip(mixed, -4.0, 4.0).astype(jnp.bfloat16)


def block_scale(stream_key, dims, cuts, smallest, high):
    gain, own = 1.0, jax.random.fold_in(stream_key, 6)
    for axis_at, parts in cuts:
        draws = jnp.exp(jax.random.uniform(jax.random.fold_in(own, axis_at), (parts,), jnp.float32, smallest / len(cuts), high / len(cuts)))
        gain = gain * jnp.repeat(draws, dims[axis_at] // parts).reshape([-1 if axis == axis_at else 1 for axis in range(len(dims))])
    return gain


def shared_out(key, own, number, rows, count, top, limit, slope):
    sequence = jax.random.permutation(key, count)
    crowded, common = portions_of(count, rows * top, limit, slope, True), portions_of(count, rows * top, limit, slope, False)
    places = jnp.arange(count)

    def named(sizes, rotation):
        used = int((sizes > 0).sum())
        fixed = max(1, used // 4)
        passed = fixed + (places - fixed + rotation * (used - fixed)) % max(1, count - fixed)
        return jnp.zeros((count,), jnp.int32).at[sequence[jnp.where(places < fixed, places, passed)]].set(jnp.asarray(sizes, jnp.int32))

    sizes = jnp.where(number % 4 == 0, named(crowded, number // 4), named(common, number - number // 4 - 1))
    mixed = jax.random.permutation(jax.random.fold_in(own, 3), count)
    source_of, sink = mixed[0:count // 2 * 2:2], mixed[1:count // 2 * 2:2]
    slack = jnp.minimum(sizes[source_of] - 1, limit - sizes[sink]) // 2
    slack = jnp.where((source_of == sequence[0]) | (sink == sequence[0]) | (sizes[sink] == 0), 0, jnp.maximum(slack, 0))
    passed = jax.random.randint(jax.random.fold_in(own, 4), (count // 2,), 0, 1 << 20) % (slack + 1)
    sizes = sizes.at[source_of].add(-passed).at[sink].add(passed)
    members = jnp.searchsorted(jnp.cumsum(sizes), jnp.arange(rows * top), side="right").astype(jnp.int32)
    table = members.reshape(top, rows).T
    table = table[jax.random.permutation(jax.random.fold_in(own, 1), rows)]
    rotation = jax.random.randint(jax.random.fold_in(own, 2), (rows, 1), 0, top)
    return jnp.take_along_axis(table, (jnp.arange(top)[None, :] + rotation) % top, axis=1)


def portions_of(amount, total, bound, slope, full):
    portions = [(1 << 20) // math.isqrt(rank ** slope) + 1 for rank in range(1, amount + 1)]
    largest = bound if full else min(bound, max(-(-total // amount), total * portions[0] // sum(portions)))
    least = 1 if total - largest >= amount - 1 else 0
    given, spare = [largest] + [least] * (amount - 1), total - largest - least * (amount - 1)
    while spare > 0:
        candidates = [i for i in range(1, amount) if given[i] < largest] or [i for i in range(1, amount) if given[i] < bound]
        mass, remaining = sum([portions[i] for i in candidates]), spare
        for i in candidates:
            extra = min(bound - given[i], max(1, remaining * portions[i] // mass), spare)
            given[i] = given[i] + extra
            spare = spare - extra
    return np.array(given)


def bell_draw(rng, shape, width, bound, cuts=(), kind=jnp.bfloat16):
    values = width * jax.random.normal(rng, shape, jnp.float32)
    if cuts:
        values = values * block_scale(rng, shape, cuts, -0.22, 0.18)
    return jnp.clip(values, -bound, bound).astype(kind)


def setup_inputs(seed: int = 0) -> dict:
    seeds = jax.random.split(jax.random.key(seed), 4)
    slots = draw_slots(jax.random.fold_in(seeds[3], 71), 0)
    slot_window_keys = jax.random.split(jax.random.fold_in(seeds[1], 1), SLOTS // SLOTS_DEV)
    slot_window_turns = jax.random.permutation(jax.random.fold_in(seeds[1], 3), SLOTS // SLOTS_DEV)
    slot_window = jax.vmap(lambda own, number: shared_out(jax.random.fold_in(seeds[1], 2), own, number, SLOTS_DEV, WINDOWS, 1, CAP, 2))(slot_window_keys, slot_window_turns).reshape((SLOTS, 1))
    first_image = bell_draw(seeds[2], (WINDOWS, DEPTH, WL * WL), 1.0, 6.0, ((0, 32), (1, 8)))
    return {"slots": slots, "slot_window": slot_window, "first_image": first_image}


def shifted_rows(cube):
    inner = WL - 2 * REACH
    rows = []
    for a in range(-REACH, REACH + 1):
        for b in range(-REACH, REACH + 1):
            for c in range(-REACH, REACH + 1):
                piece = cube[REACH + a:REACH + a + DEPTH, REACH + b:REACH + b + inner, REACH + c:REACH + c + inner]
                rows.append(piece.reshape(-1))
    return jnp.stack(rows)

def reference(slots, slot_window, first_image):
    blocks = slots.reshape(N_WIN, SLOTS_DEV, DEPTH * WL * WL)
    owners = slot_window[:, 0].reshape(N_WIN, SLOTS_DEV)

    def add_block(total, item):
        block, owner = item
        part = jax.ops.segment_sum(block.astype(jnp.float32), owner, num_segments=WINDOWS)
        part = lax.optimization_barrier(part.astype(jnp.bfloat16))
        return (total + part.astype(jnp.float32), None)
    total, _ = lax.scan(add_block, jnp.zeros((WINDOWS, DEPTH * WL * WL), jnp.float32), (blocks, owners))
    remigrated = total.astype(jnp.bfloat16).reshape(WINDOWS, DEPTH, WL, WL)
    inner = WL - 2 * REACH
    fitted = float(DEPTH * inner * inner)

    def one_window(item):
        field, target = item
        cube = jnp.pad(field.astype(jnp.float32), ((REACH, REACH), (0, 0), (0, 0)))
        rows = shifted_rows(cube)
        goal = target.reshape(DEPTH, WL, WL)[:, REACH:WL - REACH, REACH:WL - REACH].reshape(-1).astype(jnp.float32)
        gram = jnp.dot(rows, rows.T, precision=lax.Precision.HIGHEST)
        right = jnp.dot(rows, goal, precision=lax.Precision.HIGHEST)
        system = gram / fitted + 0.05 * jnp.eye(LAGS, dtype=jnp.float32)
        factor = jnp.linalg.cholesky(system)
        return jax.scipy.linalg.cho_solve((factor, True), right / jnp.sqrt(jnp.float32(fitted)))
    return lax.map(one_window, (remigrated, first_image))
```

```python
import jax
import jax.numpy as jnp
from jax import lax
from jax.experimental import pallas as pl
from jax.experimental.pallas import tpu as pltpu
from jax.sharding import PartitionSpec as P

WL = 64
REACH = 2
SPAN = 5
LAGS = 125
NX = 4
NZ = 8
OWN = 4
PLANES = 8
CELLS = WL * WL
LX = 2176
LZ = CELLS - LX
SLAB = 2176
SHIFT = CELLS - SLAB
MESH = pl.DeviceIdType.MESH
F32 = jnp.float32
BF16 = jnp.bfloat16
LATE = jnp.float32


def collect_kernel(
    table, slots, first, field_out, first_out,
    sv, xs, xr, zs, zr, qx, qz, zs2, zr2, xs2, xr2, rem,
    load_sem, xs_sem, xr_sem, zs_sem, zr_sem, zs2_sem, zr2_sem, xs2_sem, xr2_sem,
    f_send, f_recv, d_send, d_recv, self_sem,
):
    me = lax.axis_index("win")
    dep = lax.axis_index("dep")
    z, x = me // NX, lax.rem(me, NX)
    count = sv.shape[0] - 1
    load = pltpu.make_async_copy(slots, sv.at[pl.ds(0, count)], load_sem)
    load.start()

    def along_x(step):
        return z * NX + lax.rem(x + step, NX)

    def along_z(step):
        return lax.rem(z + step, NZ) * NX + x

    def dep_of(step):
        return lax.rem(dep + step, 8)

    barrier = pltpu.get_barrier_semaphore()
    for other in (along_x(1), along_x(3), along_z(1), along_z(7)):
        pl.semaphore_signal(barrier, inc=1, device_id=(other, dep), device_id_type=MESH)
    for step in range(1, 8):
        pl.semaphore_signal(barrier, inc=1, device_id=(me, dep_of(step)), device_id_type=MESH)
    pl.semaphore_wait(barrier, 11)

    def slab_copy(source, target, send, recv, step):
        to = dep_of(step)
        lanes = pl.ds(pl.multiple_of(lax.rem(to, 2) * SHIFT, 128), SLAB)
        return pltpu.make_async_remote_copy(
            source.at[to // 2, :, lanes], target.at[dep], send.at[step], recv.at[step],
            device_id=(me, to), device_id_type=MESH,
        )

    def slab_arrival(source, target, send, recv, step):
        return pltpu.make_async_remote_copy(
            source.at[0, :, pl.ds(0, SLAB)], target.at[dep_of(8 - step)], send.at[step], recv.at[step],
            device_id=(me, dep_of(step)), device_id_type=MESH,
        )

    def slab_self(source, target, sem):
        lanes = pl.ds(pl.multiple_of(lax.rem(dep, 2) * SHIFT, 128), SLAB)
        return pltpu.make_async_copy(source.at[dep // 2, :, lanes], target.at[dep], sem)

    def ring(buffer, inbox, send, recv, sideways):
        def copy(side, s):
            to = sideways(1 if side == 0 else -1)
            return pltpu.make_async_remote_copy(
                buffer.at[side, s], inbox.at[side, s], send.at[side, s], recv.at[side, s],
                device_id=(to, dep), device_id_type=MESH,
            )
        return copy

    x1 = ring(xs, xr, xs_sem, xr_sem, lambda d: along_x(1 if d > 0 else 3))
    z1 = ring(zs, zr, zs_sem, zr_sem, lambda d: along_z(1 if d > 0 else 7))
    z2 = ring(zs2, zr2, zs2_sem, zr2_sem, lambda d: along_z(1 if d > 0 else 7))
    x2 = ring(xs2, xr2, xs2_sem, xr2_sem, lambda d: along_x(1 if d > 0 else 3))

    for step in range(1, 8):
        slab_copy(first, first_out, f_send, f_recv, step).start()
    own_first = slab_self(first, first_out, self_sem.at[0])
    own_first.start()

    sv[count] = jnp.zeros(sv.shape[1:], sv.dtype)
    load.wait()

    def own(w, lo, size):
        lanes = pl.ds(lo, size)
        return sv[table[0, w], :, lanes].astype(F32) + sv[table[1, w], :, lanes].astype(F32)

    def each_window(body):
        def step(j, carry):
            body(j)
            return carry
        lax.fori_loop(0, OWN, step, 0, unroll=True)

    def x_unit(side, s, dz, step, came):
        base = (lax.rem(z + dz, NZ) * NX + lax.rem(x + step, NX)) * OWN
        if came is not None:
            x1(side, came).wait_recv()

        def body(j):
            value = own(base + j, 0, LX)
            if came is not None:
                value = value + xr[side, came, j].astype(F32)
            xs[side, s, j] = value.astype(BF16)

        each_window(body)
        x1(side, s).start()

    def z_unit(side, s, came):
        t = (s + 2) // 4
        dz = NZ // 2 - t if side == 0 else NZ // 2 + t
        xd = lax.rem(s + (0 if side == 0 else 2), 4)
        base = (lax.rem(z + dz, NZ) * NX + xd) * OWN
        if came:
            z1(side, s - 4).wait_recv()

        def body(j):
            value = own(base + j, LX, LZ)
            if came:
                value = value + zr[side, s - 4, j].astype(F32)
            zs[side, s, j] = value.astype(BF16)

        each_window(body)
        z1(side, s).start()

    def loop(lo, hi, body):
        def step(s, carry):
            body(s)
            return carry
        lax.fori_loop(lo, hi, step, 0)

    def start_both(s, came):
        x_unit(0, s, 4 + s, 2, None)
        z_unit(0, s, came)
        x_unit(1, s, 3 - s, 2, None)
        z_unit(1, s, came)

    def second(s):
        x_unit(0, s, 7 - s, 1, None)
        z_unit(0, s, True)
        x_unit(1, s, s, 3, None)
        z_unit(1, s, True)

    def third(s):
        z_unit(0, s, True)
        x_unit(0, s, s - 4, 1, s - 8)
        z_unit(1, s, True)
        x_unit(1, s, 11 - s, 3, s - 8)

    def fourth(s):
        z_unit(0, s, True)
        z_unit(1, s, True)

    loop(0, 4, lambda s: start_both(s, False))
    loop(4, 8, second)
    loop(8, 12, third)
    loop(12, 14, fourth)

    def sum_x(dz):
        r = dz + 4 if dz >= 4 else 7 - dz
        l = 11 - dz if dz < 4 else dz
        x1(0, r).wait_recv()
        x1(1, l).wait_recv()
        base = (lax.rem(z + dz, NZ) * NX + x) * OWN

        def body(j):
            qx[dz, j] = own(base + j, 0, LX) + xr[0, r, j].astype(F32) + xr[1, l, j].astype(F32)

        each_window(body)

    def z2_unit(s, came):
        for side in (0, 1):
            t = (s + 2) // 4
            dz = NZ // 2 - t if side == 0 else NZ // 2 + t
            j = lax.rem(s + (0 if side == 0 else 2), 4)
            value = qx[dz, j]
            if came:
                z2(side, s - 4).wait_recv()
                value = value + zr2[side, s - 4].astype(F32)
            zs2[side, s] = value.astype(LATE)
            z2(side, s).start()

    def sum_z(xd):
        r, l = 10 + lax.rem(xd + 2, 4), 10 + xd
        z1(0, r).wait_recv()
        z1(1, l).wait_recv()
        base = (z * NX + xd) * OWN

        def body(j):
            qz[xd, j] = own(base + j, LX, LZ) + zr[0, r, j].astype(F32) + zr[1, l, j].astype(F32)

        each_window(body)

    def x2_unit(s, came):
        for side in (0, 1):
            j = lax.rem(s + (0 if side == 0 else 2), 4)
            if s < 2:
                xd = lax.rem(x + 2, NX)
            else:
                xd = lax.rem(x + (1 if side == 0 else 3), NX)
            value = qz[xd, j]
            if came:
                x2(side, s - 4).wait_recv()
                value = value + xr2[side, s - 4].astype(F32)
            xs2[side, s] = value.astype(LATE)
            x2(side, s).start()

    sum_x(4)
    loop(0, 2, lambda s: z2_unit(s, False))
    sum_x(3)
    sum_x(5)
    loop(2, 4, lambda s: z2_unit(s, False))
    loop(0, NX, sum_z)
    for s in range(4):
        x2_unit(s, False)
    loop(4, 6, lambda s: z2_unit(s, True))
    for s in range(4, 6):
        x2_unit(s, True)
    sum_x(2)
    sum_x(6)
    loop(6, 10, lambda s: z2_unit(s, True))
    sum_x(1)
    sum_x(7)
    loop(10, 14, lambda s: z2_unit(s, True))
    sum_x(0)

    def finish(j):
        r, l = 2 + lax.rem(j + 2, 4), 2 + j
        x2(0, r).wait_recv()
        x2(1, l).wait_recv()
        value = qz[x, j] + xr2[0, r].astype(F32) + xr2[1, l].astype(F32)
        rem[j, :, LX:] = value.astype(BF16)
        r, l = 10 + lax.rem(j + 2, 4), 10 + j
        z2(0, r).wait_recv()
        z2(1, l).wait_recv()
        value = qx[0, j] + zr2[0, r].astype(F32) + zr2[1, l].astype(F32)
        rem[j, :, :LX] = value.astype(BF16)

    loop(0, OWN, finish)
    for step in range(1, 8):
        slab_copy(rem, field_out, d_send, d_recv, step).start()
    own_field = slab_self(rem, field_out, self_sem.at[1])
    own_field.start()

    def drain(copy, number):
        def step(s):
            copy(0, s).wait_send()
            copy(1, s).wait_send()
        loop(0, number, step)

    drain(x1, 12)
    drain(z1, 14)
    drain(z2, 14)
    drain(x2, 6)
    own_first.wait()
    own_field.wait()
    for step in range(1, 8):
        slab_copy(first, first_out, f_send, f_recv, step).wait_send()
        slab_arrival(first, first_out, f_send, f_recv, step).wait_recv()
        slab_copy(rem, field_out, d_send, d_recv, step).wait_send()
        slab_arrival(rem, field_out, d_send, d_recv, step).wait_recv()


def collect(table, slots, first):
    count = slots.shape[0]
    dma = pltpu.SemaphoreType.DMA
    slab = jax.ShapeDtypeStruct((8, PLANES, SLAB), BF16)
    return pl.pallas_call(
        collect_kernel,
        out_shape=(slab, slab),
        in_specs=[
            pl.BlockSpec(memory_space=pltpu.SMEM),
            pl.BlockSpec(memory_space=pl.ANY),
            pl.BlockSpec(memory_space=pl.ANY),
        ],
        out_specs=(pl.BlockSpec(memory_space=pl.ANY), pl.BlockSpec(memory_space=pl.ANY)),
        scratch_shapes=[
            pltpu.VMEM((count + 1, PLANES, CELLS), BF16),
            pltpu.VMEM((2, 12, OWN, PLANES, LX), BF16),
            pltpu.VMEM((2, 12, OWN, PLANES, LX), BF16),
            pltpu.VMEM((2, 14, OWN, PLANES, LZ), BF16),
            pltpu.VMEM((2, 14, OWN, PLANES, LZ), BF16),
            pltpu.VMEM((NZ, OWN, PLANES, LX), F32),
            pltpu.VMEM((NX, OWN, PLANES, LZ), F32),
            pltpu.VMEM((2, 14, PLANES, LX), LATE),
            pltpu.VMEM((2, 14, PLANES, LX), LATE),
            pltpu.VMEM((2, 6, PLANES, LZ), LATE),
            pltpu.VMEM((2, 6, PLANES, LZ), LATE),
            pltpu.VMEM((OWN, PLANES, CELLS), BF16),
            dma, dma((2, 12)), dma((2, 12)), dma((2, 14)), dma((2, 14)),
            dma((2, 14)), dma((2, 14)), dma((2, 6)), dma((2, 6)),
            dma((8,)), dma((8,)), dma((8,)), dma((8,)), dma((2,)),
        ],
        compiler_params=pltpu.CompilerParams(
            collective_id=0, has_side_effects=True, vmem_limit_bytes=60 * 1024 * 1024
        ),
        name="collect",
    )(table, slots, first)


ROWS = 26 * 16
KLANES = 1920


def normal_kernel(field, first, out, pad, fpad, shifted, total):
    pad[...] = jnp.zeros_like(pad)
    fpad[...] = jnp.zeros_like(fpad)
    for d in range(8):
        pad[pl.ds(REACH + 8 * d, 8), :] = field[d].astype(F32)
    lane = lax.broadcasted_iota(jnp.int32, (16, SLAB), 1)
    column = lax.rem(lane, WL)
    inside = (column >= REACH) & (column < WL - REACH)
    total[...] = jnp.zeros_like(total)

    def group(g, carry):
        start = pl.multiple_of(8 * g, 8)
        planes = pad[pl.ds(start, 16), :]
        for c in range(-REACH, REACH + 1):
            moved = planes if c == 0 else pltpu.roll(planes, (-c) % SLAB, 1)
            moved = jnp.where(inside, moved, 0.0)
            half = pltpu.roll(moved, SLAB - WL, 1).astype(BF16)
            moved = moved.astype(BF16)
            for b in range(-REACH, REACH + 1):
                at = 16 * ((b + REACH) * SPAN + c + REACH)
                lo = 128 + WL * b
                if b % 2 == 0:
                    shifted[pl.ds(at, 16), :] = moved[:, lo:lo + KLANES]
                else:
                    shifted[pl.ds(at, 16), :] = half[:, lo - WL:lo - WL + KLANES]
        fpad[pl.ds(0, 8), :] = first[g].astype(F32)
        shifted[pl.ds(400, 16), :] = fpad[:, 128:128 + KLANES].astype(BF16)
        rows = shifted[...]
        total[...] += lax.dot_general(
            rows, rows, (((1,), (1,)), ((), ())), preferred_element_type=F32
        )
        return carry

    lax.fori_loop(0, 8, group, 0)

    value = total[...]
    for step in (1, 2, 4):
        value = value + pltpu.roll(pltpu.roll(value, ROWS - step, 0), ROWS - step, 1)
    lag = lax.broadcasted_iota(jnp.int32, (128, ROWS), 0)
    row = lax.broadcasted_iota(jnp.int32, (128, ROWS), 1)
    source = jnp.where(lag < LAGS, 16 * lax.rem(lag, 25) + lag // 25, 400)
    pick = jnp.where((source == row) & (lag <= LAGS), 1.0, 0.0)
    half = lax.dot_general(
        pick, value, (((1,), (0,)), ((), ())),
        precision=lax.Precision.HIGHEST, preferred_element_type=F32,
    )
    out[...] = lax.dot_general(
        half, pick, (((1,), (1,)), ((), ())),
        precision=lax.Precision.HIGHEST, preferred_element_type=F32,
    )


def normal(field, first):
    vmem = pl.BlockSpec(memory_space=pltpu.VMEM)
    return pl.pallas_call(
        normal_kernel,
        out_shape=jax.ShapeDtypeStruct((128, 128), F32),
        in_specs=[vmem, vmem],
        out_specs=vmem,
        scratch_shapes=[
            pltpu.VMEM((80, SLAB), F32),
            pltpu.VMEM((16, SLAB), F32),
            pltpu.VMEM((ROWS, KLANES), BF16),
            pltpu.VMEM((ROWS, ROWS), F32),
        ],
        compiler_params=pltpu.CompilerParams(vmem_limit_bytes=40 * 1024 * 1024),
        name="normal",
    )(field, first)


def pair_kernel(mine, out, inbox, send_sem, recv_sem):
    me = lax.axis_index("win")
    dep = lax.axis_index("dep")
    other = dep + 1 - 2 * lax.rem(dep, 2)
    barrier = pltpu.get_barrier_semaphore()
    pl.semaphore_signal(barrier, inc=1, device_id=(me, other), device_id_type=MESH)
    pl.semaphore_wait(barrier, 1)
    copy = pltpu.make_async_remote_copy(
        mine, inbox, send_sem, recv_sem, device_id=(me, other), device_id_type=MESH
    )
    copy.start()
    copy.wait()
    out[...] = mine[...] + inbox[...]


def pair(mine):
    vmem = pl.BlockSpec(memory_space=pltpu.VMEM)
    return pl.pallas_call(
        pair_kernel,
        out_shape=jax.ShapeDtypeStruct((128, 128), F32),
        in_specs=[vmem],
        out_specs=vmem,
        scratch_shapes=[
            pltpu.VMEM((128, 128), F32), pltpu.SemaphoreType.DMA, pltpu.SemaphoreType.DMA,
        ],
        compiler_params=pltpu.CompilerParams(collective_id=1, has_side_effects=True),
        name="pair",
    )(mine)


def solve_kernel(fitted, gram, out):
    row = lax.broadcasted_iota(jnp.int32, (128, 128), 0)
    lane = lax.broadcasted_iota(jnp.int32, (128, 128), 1)
    value = gram[...]
    scaled = value / fitted + jnp.where(row == lane, 0.05, 0.0)
    value = jnp.where(row == LAGS, value / jnp.sqrt(jnp.float32(fitted)), scaled)
    lanes = lax.broadcasted_iota(jnp.int32, (1, 128), 1)
    done = 0
    for k in range(LAGS):
        if k // 8 * 8 > done:
            value = value[k // 8 * 8 - done:]
            done = k // 8 * 8
        at = k - done
        column = value[:, k:k + 1]
        pivot = value[at:at + 1, :]
        scale = 1.0 / value[at:at + 1, k:k + 1]
        pivot = jnp.where(lanes == k, -scale, pivot * scale)
        value = jnp.where(lanes == k, 0.0, value) - column * pivot
    out[...] = jnp.broadcast_to(value[LAGS - done:LAGS - done + 1, :], (8, 128))


def solve(gram, fitted):
    vmem = pl.BlockSpec(memory_space=pltpu.VMEM)
    return pl.pallas_call(
        lambda gram, out: solve_kernel(fitted, gram, out),
        out_shape=jax.ShapeDtypeStruct((8, 128), F32),
        in_specs=[vmem],
        out_specs=vmem,
        name="solve",
    )(gram)


def gather_kernel(mine, out, inbox, send_sem, recv_sem):
    me = lax.axis_index("win")
    dep = lax.axis_index("dep")
    y = dep // 2

    def peer(step):
        return lax.rem(dep + 2 * step, 8)

    barrier = pltpu.get_barrier_semaphore()
    for step in (1, 2, 3):
        pl.semaphore_signal(barrier, inc=1, device_id=(me, peer(step)), device_id_type=MESH)
    pl.semaphore_wait(barrier, 3)

    def copy(step):
        return pltpu.make_async_remote_copy(
            mine, inbox.at[step], send_sem.at[step], recv_sem.at[step],
            device_id=(me, peer(step)), device_id_type=MESH,
        )

    for step in (1, 2, 3):
        copy(step).start()
    out[pl.ds(y, 1), :] = mine[pl.ds(0, 1), :]
    for step in (1, 2, 3):
        copy(step).wait()
        out[pl.ds(lax.rem(y + 4 - step, 4), 1), :] = inbox[step, pl.ds(0, 1), :]


def gather(mine):
    vmem = pl.BlockSpec(memory_space=pltpu.VMEM)
    return pl.pallas_call(
        gather_kernel,
        out_shape=jax.ShapeDtypeStruct((OWN, 128), F32),
        in_specs=[vmem],
        out_specs=vmem,
        scratch_shapes=[
            pltpu.VMEM((4, 8, 128), F32),
            pltpu.SemaphoreType.DMA((4,)), pltpu.SemaphoreType.DMA((4,)),
        ],
        compiler_params=pltpu.CompilerParams(collective_id=2, has_side_effects=True),
        name="gather",
    )(mine)


def per_device(slots, slot_window, first_image):
    count = slots.shape[0]
    names = slot_window[:, 0]
    places = jnp.arange(count, dtype=jnp.int32)
    named = names[None, :] == jnp.arange(128, dtype=jnp.int32)[:, None]
    low = jnp.min(jnp.where(named, places[None, :], count), axis=1)
    high = jnp.max(jnp.where(named, places[None, :], -1), axis=1)
    table = jnp.stack([low, jnp.where(high > low, high, count)])
    field, first = collect(table, slots, first_image)
    fitted = float(64 * (WL - 2 * REACH) ** 2)
    gram = pair(normal(field, first))
    return gather(solve(gram, fitted))[:, :LAGS]


def solution(mesh):
    return jax.shard_map(
        per_device,
        mesh=mesh,
        in_specs=(P("win", "dep", None), P("win", None), P("win", "dep", None)),
        out_specs=P("win", None),
        check_vma=False,
    )
```
